32 devices in a mesh: cand: 8 (over y, x, core), row: 4 (over z).
Axes of the slice: x: 2, y: 2, z: 4, core: 2. Of those that a mesh axis runs over, the one named last changes fastest.
Arguments:
- right_side: bfloat16 [16384, 8192], P('row', 'cand'), may hold values from -6 to 6
- factor_panel: bfloat16 [4, 4096, 1024], P('row', 'cand'), may hold values from -6 to 6
- diag_inverse: float32 [2, 512, 512], replicated, as said below
- prior_variance: float32 [8192], P('cand'), may hold values from 12 to 20
- block_index: int32 [1], replicated, may hold values from 0 to 30
Outputs:
- solved_side: bfloat16 [16384, 8192], P('row', 'cand')
- variance: float32 [8192], P('cand')
The draws below stay inside these ranges and needn't reach their ends.
Inputs may be any that keep to these rules, and one draw needn't show every extreme that they name: Each diag_inverse[s] is lower triangular with positive diagonal. Blocks block_index[0] .. block_index[0] + 1 lie inside the window.
All inputs are finite; a program needn't handle non-finite values.
Results may differ from the reference program's by a relative error of at most 0.0037.
Values may be sent and summed in bfloat16 or wider, within the bound.
A program may use at most 128 MiB of HBM per device.

```python
import math
import jax
import jax.numpy as jnp
from jax import lax

BLK = 512
STEPS = 2
NB_DEV = 8
ROWS_DEV = 4096
ROWS = 16384
CANDS = 8192
N_ROW = 4


def draw_diag_inverse(key, part):
    key_off = jax.random.fold_in(key, 11)
    key_diag = jax.random.fold_in(key, 12)
    full_shape = (STEPS, BLK, BLK)
    spread = jax.random.normal(key_off, full_shape, jnp.float32)
    diagonal = jnp.exp(jax.random.uniform(key_diag, full_shape, jnp.float32, -0.6931, 0.6931))
    row_iota = lax.broadcasted_iota(jnp.int32, full_shape, 1)
    col_iota = lax.broadcasted_iota(jnp.int32, full_shape, 2)
    below_diag = jnp.where(row_iota > col_iota, spread * (0.5 / math.sqrt(BLK)), 0.0)
    return jnp.where(row_iota == col_iota, diagonal, below_diag) / math.sqrt(BLK)


def shard_levels(rng, dims, cuts, low, top_value):
    def one(position, shards_of):
        steps = jax.random.uniform(jax.random.fold_in(jax.random.fold_in(rng, 6), position), (shards_of,), jnp.float32, low / len(cuts), top_value / len(cuts))
        return jnp.repeat(jnp.exp(steps), dims[position] // shards_of).reshape((-1,) + (1,) * (len(dims) - position - 1))

    loudness = one(*cuts[0])
    for cut in cuts[1:]:
        loudness = loudness * one(*cut)
    return loudness


def centred(rng, dims, scale, limit, pieces=(), held_as=jnp.bfloat16):
    values = scale * jax.random.normal(rng, dims, jnp.float32)
    if pieces:
        values = values * shard_levels(rng, dims, pieces, -0.22, 0.18)
    return jnp.clip(values, -limit, limit).astype(held_as)


def setup_inputs(seed: int = 0) -> dict:
    streams_of = jax.random.split(jax.random.key(seed), 6)
    return {
        "right_side": centred(streams_of[0], (ROWS, CANDS), 1.0, 6.0, ((0, 4), (1, 8))),
        "factor_panel": centred(streams_of[1], (N_ROW, ROWS_DEV, STEPS * BLK), 1.0, 6.0, ((0, 4), (1, 8))),
        "diag_inverse": draw_diag_inverse(jax.random.fold_in(streams_of[5], 71), 0),
        "prior_variance": jnp.clip(12.0 + 8.0 * jax.random.uniform(streams_of[3], (CANDS,), jnp.float32) ** shard_levels(streams_of[3], (CANDS,), ((0, 8),), -0.2, 0.2), 12.0, 20.0),
        "block_index": jax.random.randint(streams_of[4], (1,), 0, NB_DEV * N_ROW - STEPS + 1).astype(jnp.int32),
    }


def reference(right_side, factor_panel, diag_inverse, prior_variance, block_index):
    first = block_index[0]
    working = right_side.astype(jnp.float32)
    columns_all = factor_panel.reshape(ROWS, STEPS * BLK)
    row_block = (jnp.arange(ROWS, dtype=jnp.int32) // BLK)[:, None]
    variance = prior_variance
    for step in range(STEPS):
        current = first + step
        start = (current * BLK).astype(jnp.int32)
        pending = lax.dynamic_slice_in_dim(working, start, BLK, 0)
        solved = jnp.dot(diag_inverse[step], pending, precision=lax.Precision.HIGHEST, preferred_element_type=jnp.float32)
        variance = variance - jnp.sum(solved * solved, axis=0)
        column = columns_all[:, step * BLK:(step + 1) * BLK]
        update = jnp.dot(column, solved.astype(jnp.bfloat16), preferred_element_type=jnp.float32)
        working = jnp.where(row_block > current, working - update, working)
        working = lax.dynamic_update_slice_in_dim(working, solved, start, 0)
    return working.astype(jnp.bfloat16), variance
```

```python
import functools

import jax
import jax.numpy as jnp
from jax import lax
from jax.experimental import pallas as pl
from jax.experimental.pallas import tpu as pltpu
from jax.sharding import PartitionSpec as P

MESH = pl.DeviceIdType.MESH
HALVES = 2


def bits_of(value):
    return [1 << b for b in range(value.bit_length()) if value >> b & 1]


def last_hop(rel, half):
    bits = bits_of(rel)
    if rel & 1 or half:
        return bits[0]
    return bits[-1]


def kernel(
    n_cand,
    n_row,
    chunk,
    right_ref,
    factor_ref,
    diag_ref,
    prior_ref,
    index_ref,
    out_ref,
    var_ref,
    rows_buf,
    fac_first,
    fac_second,
    out_buf,
    solved,
    arrived,
    diag_f32,
    diag_hi,
    diag_lo,
    level,
    cross,
    square,
    square_in,
    load_sem,
    store_sem,
    f_send,
    f_recv,
    z_send,
    z_recv,
    v_send,
    v_recv,
):
    fac = (fac_first, fac_second)
    rows_dev = rows_buf.shape[0]
    steps, blk = diag_f32.shape[0], diag_f32.shape[1]
    blocks_dev = rows_dev // blk
    n_chunk = solved.shape[1]
    own_rows = factor_ref.shape[1]
    half_rows = own_rows // 2
    z_rows = blk // HALVES
    me = lax.axis_index("cand")
    row = lax.axis_index("row")
    dims = [1 << b for b in range((n_cand - 1).bit_length())]

    def device_at(rel):
        return me + sum(b * (1 - 2 * ((me // b) % 2)) for b in bits_of(rel))

    load_rows = pltpu.make_async_copy(right_ref, rows_buf, load_sem.at[0])
    load_diag = pltpu.make_async_copy(diag_ref, diag_f32, load_sem.at[1])
    load_diag.start()
    load_rows.start()
    own_copies = []
    for s in range(steps):
        cp = pltpu.make_async_copy(
            factor_ref.at[0, :, pl.ds(s * blk, blk)],
            fac[s].at[pl.ds(pl.multiple_of(me * own_rows, own_rows), own_rows)],
            load_sem.at[2 + s],
        )
        cp.start()
        own_copies.append(cp)

    barrier = pltpu.get_barrier_semaphore()
    for d in dims:
        pl.semaphore_signal(barrier, inc=1, device_id=(device_at(d), row), device_id_type=MESH)
    for k in range(1, n_row):
        other = lax.rem(row + k, n_row)
        pl.semaphore_signal(barrier, inc=1, device_id=(me, other), device_id_type=MESH)
    pl.semaphore_wait(barrier, len(dims) + n_row - 1)

    def piece_rows(rel, half):
        start = device_at(rel) * own_rows + half * half_rows
        return pl.ds(pl.multiple_of(start, half_rows), half_rows)

    def f_copy(s, rel, half):
        dim = last_hop(rel, half)
        held = rel ^ dim
        dst = fac[s].at[piece_rows(held, half)]
        if held == 0:
            src = factor_ref.at[0, pl.ds(half * half_rows, half_rows), pl.ds(s * blk, blk)]
        else:
            src = dst
        return pltpu.make_async_remote_copy(
            src_ref=src,
            dst_ref=dst,
            send_sem=f_send.at[s, rel, half],
            recv_sem=f_recv.at[s, rel, half],
            device_id=(device_at(dim), row),
            device_id_type=MESH,
        )

    def f_arrival(s, rel, half):
        dim = last_hop(rel, half)
        dst = fac[s].at[piece_rows(rel, half)]
        return pltpu.make_async_remote_copy(
            src_ref=dst,
            dst_ref=dst,
            send_sem=f_send.at[s, rel, half],
            recv_sem=f_recv.at[s, rel, half],
            device_id=(device_at(dim), row),
            device_id_type=MESH,
        )

    def f_start_own(s):
        for turn in range(2):
            for i, d in enumerate(reversed(dims)):
                half = turn if d == 2 or d == 1 else 1 - turn
                f_copy(s, d, half).start()

    forwards = [
        (rel, half)
        for rel in range(1, n_cand)
        if len(bits_of(rel)) > 1
        for half in range(2)
    ]

    def f_pass_on(s, rel, half):
        f_arrival(s, rel, half).wait_recv()
        nexts = [q for q, h in forwards if h == half and q ^ last_hop(q, h) == rel]
        for q in sorted(nexts, key=lambda q: q & 1):
            f_copy(s, q, half).start()

    singles = [d for d in dims if d > 1]
    waited = {(d, h) for d in singles for h in range(2)}

    def f_action(s, number):
        if number == 0:
            for d in singles:
                f_pass_on(s, d, 0 if d == 2 else 1)
        elif number == 1:
            for d in singles:
                f_pass_on(s, d, 1 if d == 2 else 0)
        elif number == 2:
            relays = [q for q in range(2, n_cand, 2) if len(bits_of(q)) > 1]
            for q in sorted(relays, key=lambda q: len(bits_of(q))):
                for half in range(2):
                    waited.add((q, half))
                    f_pass_on(s, q, half)
        else:
            for rel in range(1, n_cand):
                for half in range(2):
                    if (rel, half) not in waited:
                        f_arrival(s, rel, half).wait_recv()

    f_start_own(0)

    place = jnp.clip(index_ref[0] - row * blocks_dev, -2, blocks_dev).astype(jnp.float32)
    level[...] = jnp.full(level.shape, place).astype(jnp.bfloat16)

    def at(width):
        return level[:, :width]

    def own(s, value, other):
        here = level[: value.shape[0], : value.shape[1]].astype(value.dtype)
        inside = jnp.where(here < blocks_dev - s, value, other)
        return jnp.where(here >= -s, inside, other)

    def block_of(ref, s, cols):
        value = ref[:blk, cols]
        for b in range(1, blocks_dev):
            value = jnp.where(at(value.shape[1]) == b - s, ref[b * blk : (b + 1) * blk, cols], value)
        return value

    def z_copy(s, j, half):
        part = pl.ds(half * z_rows, z_rows)
        return pltpu.make_async_remote_copy(
            src_ref=solved.at[s, j, part],
            dst_ref=arrived.at[s, j, part],
            send_sem=z_send.at[s, j, half],
            recv_sem=z_recv.at[s, j, half],
            device_id=(me, lax.rem(row + 1, n_row)),
            device_id_type=MESH,
        )

    def z_send_on(s, j, half):
        @pl.when(row < n_row - 1)
        def _():
            z_copy(s, j, half).start()

    def z_take(s, j, half):
        part = pl.ds(half * z_rows, z_rows)

        @pl.when(row > 0)
        def _():
            z_copy(s, j, half).wait_recv()
            solved[s, j, part, :] = own(s, solved[s, j, part, :], arrived[s, j, part, :])

    def dot(a, b):
        return jnp.dot(a, b, preferred_element_type=jnp.float32)

    def add_squares(s, j, value):
        sums = jnp.sum((value * value).reshape(blk // 8, 8, chunk), axis=0)
        square[j] = square[j] + own(s, sums, jnp.zeros_like(sums))

    load_diag.wait()
    for s in range(steps):
        full = diag_f32[s]
        high = full.astype(jnp.bfloat16)
        diag_hi[s] = high
        diag_lo[s] = (full - high.astype(jnp.float32)).astype(jnp.bfloat16)
    square[...] = jnp.zeros_like(square)
    load_rows.wait()

    def columns(j):
        return slice(j * chunk, (j + 1) * chunk)

    for j in range(n_chunk):
        pending = block_of(rows_buf, 0, columns(j))
        value = dot(diag_hi[0], pending) + dot(diag_lo[0], pending)
        solved[0, j] = value.astype(jnp.bfloat16)
        add_squares(0, j, value)

        @pl.when(row == 0)
        def _():
            for half in range(HALVES):
                z_copy(0, j, half).start()

    for cp in own_copies:
        cp.wait()

    def z_later(s, j, half):
        @pl.when(jnp.logical_and(row > 0, row < n_row - 1))
        def _():
            z_copy(s, j, half).start()

    z_units = n_chunk * HALVES

    for k in range(z_units):
        j, half = k // HALVES, k % HALVES
        z_take(0, j, half)
        z_later(0, j, half)
        if k == 0:
            f_action(0, 0)
        if k == z_units // 4:
            f_action(0, 1)
            f_start_own(1)
        if k == z_units // 2:
            f_action(0, 2)
    f_action(0, 3)
    cross[...] = block_of(fac[0], 1, slice(0, blk))

    def candidate(s, j):
        update = dot(cross[...], solved[0, j])
        pending = block_of(rows_buf, s, columns(j)).astype(jnp.float32) - update
        high = pending.astype(jnp.bfloat16)
        low = (pending - high.astype(jnp.float32)).astype(jnp.bfloat16)
        value = dot(diag_hi[s], high) + (dot(diag_lo[s], high) + dot(diag_hi[s], low))
        solved[s, j] = value.astype(jnp.bfloat16)
        add_squares(s, j, value)

    def finish(j):
        def body(b, _):
            rows = pl.ds(pl.multiple_of(b * blk, blk), blk)
            below = jnp.full((blk, chunk), b.astype(jnp.float32)).astype(jnp.bfloat16) - at(chunk)
            base = rows_buf[rows, columns(j)]
            update = dot(fac[0][rows, :], solved[0, j]) + dot(fac[1][rows, :], solved[1, j])
            moved = (base.astype(jnp.float32) - update).astype(jnp.bfloat16)
            value = jnp.where(below > 1, moved, base)
            value = jnp.where(below == 0, solved[0, j], value)
            value = jnp.where(below == 1, solved[1, j], value)
            out_buf[rows, columns(j)] = value
            return 0

        for part in range(2):
            lax.fori_loop(part * blocks_dev // 2, (part + 1) * blocks_dev // 2, body, 0)
            store(j, part).start()

    def store(j, part):
        rows = pl.ds(part * rows_dev // 2, rows_dev // 2)
        cols = pl.ds(j * chunk, chunk)
        return pltpu.make_async_copy(
            out_buf.at[rows, cols], out_ref.at[rows, cols], store_sem.at[j, part]
        )

    def v_copy(k):
        return pltpu.make_async_remote_copy(
            src_ref=square,
            dst_ref=square_in.at[k - 1],
            send_sem=v_send.at[k - 1],
            recv_sem=v_recv.at[k - 1],
            device_id=(me, lax.rem(row + k, n_row)),
            device_id_type=MESH,
        )

    done = 0
    for k in range(z_units):
        j, half = k // HALVES, k % HALVES
        if half == 0:
            candidate(1, j)
        z_take(1, j, half)
        z_send_on(1, j, half)
        if k == 0:
            f_action(1, 0)
        if k == z_units // 8:
            f_action(1, 1)
        if k == 3 * z_units // 8:
            f_action(1, 2)
        if k == z_units // 2:
            f_action(1, 3)
        if k == z_units - HALVES:
            for other in range(1, n_row):
                v_copy(other).start()
        if k >= z_units // 2:
            while done < j and done <= k - z_units // 2:
                finish(done)
                done += 1
    while done < n_chunk:
        finish(done)
        done += 1

    total = square[...]
    for other in range(1, n_row):
        v_copy(other).wait_recv()
        total = total + square_in[other - 1]
    for j in range(n_chunk):
        var_ref[:, columns(j)] = prior_ref[:, columns(j)] - jnp.sum(total[j], axis=0, keepdims=True)

    for s in range(steps):
        for rel in range(1, n_cand):
            for half in range(2):
                f_copy(s, rel, half).wait_send()

    @pl.when(row < n_row - 1)
    def _():
        for s in range(steps):
            for k in range(z_units):
                z_copy(s, k // HALVES, k % HALVES).wait_send()

    for other in range(1, n_row):
        v_copy(other).wait_send()
    for j in range(n_chunk):
        for part in range(2):
            store(j, part).wait()


def shards(n_cand, n_row, right_side, factor_panel, diag_inverse, prior_variance, block_index):
    rows_dev, cands = right_side.shape
    steps, blk = diag_inverse.shape[:2]
    chunk = 256
    n_chunk = cands // chunk
    bf16, f32 = jnp.bfloat16, jnp.float32
    any_space = pl.BlockSpec(memory_space=pl.ANY)
    vmem = pl.BlockSpec(memory_space=pltpu.VMEM)
    dma = pltpu.SemaphoreType.DMA
    out, variance = pl.pallas_call(
        functools.partial(kernel, n_cand, n_row, chunk),
        out_shape=(
            jax.ShapeDtypeStruct((rows_dev, cands), bf16),
            jax.ShapeDtypeStruct((1, cands), f32),
        ),
        in_specs=[any_space, any_space, any_space, vmem, pl.BlockSpec(memory_space=pltpu.SMEM)],
        out_specs=(any_space, vmem),
        scratch_shapes=[
            pltpu.VMEM((rows_dev, cands), bf16),
            pltpu.VMEM((rows_dev, blk), bf16),
            pltpu.VMEM((rows_dev, blk), bf16),
            pltpu.VMEM((rows_dev, cands), bf16),
            pltpu.VMEM((steps, n_chunk, blk, chunk), bf16),
            pltpu.VMEM((steps, n_chunk, blk, chunk), bf16),
            pltpu.VMEM((steps, blk, blk), f32),
            pltpu.VMEM((steps, blk, blk), bf16),
            pltpu.VMEM((steps, blk, blk), bf16),
            pltpu.VMEM((blk, blk), bf16),
            pltpu.VMEM((blk, blk), bf16),
            pltpu.VMEM((n_chunk, 8, chunk), f32),
            pltpu.VMEM((n_row - 1, n_chunk, 8, chunk), f32),
            dma((2 + steps,)),
            dma((n_chunk, 2)),
            dma((steps, n_cand, 2)),
            dma((steps, n_cand, 2)),
            dma((steps, n_chunk, HALVES)),
            dma((steps, n_chunk, HALVES)),
            dma((n_row - 1,)),
            dma((n_row - 1,)),
        ],
        compiler_params=pltpu.CompilerParams(
            collective_id=0, has_side_effects=True, vmem_limit_bytes=56 << 20
        ),
        cost_estimate=pl.CostEstimate(
            flops=2 * rows_dev * cands * steps * blk, bytes_accessed=32 << 20, transcendentals=0
        ),
        name="block_steps",
    )(right_side, factor_panel, diag_inverse, prior_variance.reshape(1, cands), block_index)
    return out, variance.reshape(cands)


def solution(mesh):
    return jax.shard_map(
        functools.partial(shards, mesh.shape["cand"], mesh.shape["row"]),
        mesh=mesh,
        in_specs=(P("row", "cand"), P("row", "cand", None), P(), P("cand"), P()),
        out_specs=(P("row", "cand"), P("cand")),
        check_vma=False,
    )
```

```python
import functools

import jax
import jax.numpy as jnp
from jax import lax
from jax.experimental import pallas as pl
from jax.experimental.pallas import tpu as pltpu
from jax.sharding import PartitionSpec as P

MESH = pl.DeviceIdType.MESH
HALVES = 2


def bits_of(value):
    return [1 << b for b in range(value.bit_length()) if value >> b & 1]


def last_hop(rel, half):
    bits = bits_of(rel)
    if rel & 1 or half:
        return bits[0]
    return bits[-1]


def kernel(
    n_cand,
    n_row,
    chunk,
    right_ref,
    factor_ref,
    diag_ref,
    prior_ref,
    index_ref,
    out_ref,
    var_ref,
    rows_buf,
    fac_first,
    fac_second,
    solved,
    arrived,
    diag_f32,
    diag_hi,
    diag_lo,
    level,
    cross,
    square,
    square_in,
    load_sem,
    f_send,
    f_recv,
    z_send,
    z_recv,
    v_send,
    v_recv,
):
    fac = (fac_first, fac_second)
    rows_dev = rows_buf.shape[0]
    steps, blk = diag_f32.shape[0], diag_f32.shape[1]
    blocks_dev = rows_dev // blk
    n_chunk = solved.shape[1]
    own_rows = factor_ref.shape[1]
    half_rows = own_rows // 2
    z_rows = blk // HALVES
    me = lax.axis_index("cand")
    row = lax.axis_index("row")
    dims = [1 << b for b in range((n_cand - 1).bit_length())]

    def device_at(rel):
        return me + sum(b * (1 - 2 * ((me // b) % 2)) for b in bits_of(rel))

    load_rows = pltpu.make_async_copy(right_ref, rows_buf, load_sem.at[0])
    load_diag = pltpu.make_async_copy(diag_ref, diag_f32, load_sem.at[1])
    load_diag.start()
    load_rows.start()
    own_copies = []
    for s in range(steps):
        cp = pltpu.make_async_copy(
            factor_ref.at[0, :, pl.ds(s * blk, blk)],
            fac[s].at[pl.ds(pl.multiple_of(me * own_rows, own_rows), own_rows)],
            load_sem.at[2 + s],
        )
        cp.start()
        own_copies.append(cp)

    barrier = pltpu.get_barrier_semaphore()
    for d in dims:
        pl.semaphore_signal(barrier, inc=1, device_id=(device_at(d), row), device_id_type=MESH)
    for k in range(1, n_row):
        other = lax.rem(row + k, n_row)
        pl.semaphore_signal(barrier, inc=1, device_id=(me, other), device_id_type=MESH)
    pl.semaphore_wait(barrier, len(dims) + n_row - 1)

    def piece_rows(rel, half):
        start = device_at(rel) * own_rows + half * half_rows
        return pl.ds(pl.multiple_of(start, half_rows), half_rows)

    def f_copy(s, rel, half):
        dim = last_hop(rel, half)
        held = rel ^ dim
        dst = fac[s].at[piece_rows(held, half)]
        if held == 0:
            src = factor_ref.at[0, pl.ds(half * half_rows, half_rows), pl.ds(s * blk, blk)]
        else:
            src = dst
        return pltpu.make_async_remote_copy(
            src_ref=src,
            dst_ref=dst,
            send_sem=f_send.at[s, rel, half],
            recv_sem=f_recv.at[s, rel, half],
            device_id=(device_at(dim), row),
            device_id_type=MESH,
        )

    def f_arrival(s, rel, half):
        dim = last_hop(rel, half)
        dst = fac[s].at[piece_rows(rel, half)]
        return pltpu.make_async_remote_copy(
            src_ref=dst,
            dst_ref=dst,
            send_sem=f_send.at[s, rel, half],
            recv_sem=f_recv.at[s, rel, half],
            device_id=(device_at(dim), row),
            device_id_type=MESH,
        )

    def f_start_own(s):
        for turn in range(2):
            for i, d in enumerate(reversed(dims)):
                half = turn if d == 2 or d == 1 else 1 - turn
                f_copy(s, d, half).start()

    forwards = [
        (rel, half)
        for rel in range(1, n_cand)
        if len(bits_of(rel)) > 1
        for half in range(2)
    ]

    def f_pass_on(s, rel, half):
        f_arrival(s, rel, half).wait_recv()
        nexts = [q for q, h in forwards if h == half and q ^ last_hop(q, h) == rel]
        for q in sorted(nexts, key=lambda q: q & 1):
            f_copy(s, q, half).start()

    singles = [d for d in dims if d > 1]
    waited = {(d, h) for d in singles for h in range(2)}

    def f_action(s, number):
        if number == 0:
            for d in singles:
                f_pass_on(s, d, 0 if d == 2 else 1)
        elif number == 1:
            for d in singles:
                f_pass_on(s, d, 1 if d == 2 else 0)
        elif number == 2:
            relays = [q for q in range(2, n_cand, 2) if len(bits_of(q)) > 1]
            for q in sorted(relays, key=lambda q: len(bits_of(q))):
                for half in range(2):
                    waited.add((q, half))
                    f_pass_on(s, q, half)
        else:
            for rel in range(1, n_cand):
                for half in range(2):
                    if (rel, half) not in waited:
                        f_arrival(s, rel, half).wait_recv()

    f_start_own(0)

    place = jnp.clip(index_ref[0] - row * blocks_dev, -2, blocks_dev).astype(jnp.float32)
    level[...] = jnp.full(level.shape, place).astype(jnp.bfloat16)

    def at(width):
        return level[:, :width]

    def own(s, value, other):
        here = level[: value.shape[0], : value.shape[1]].astype(value.dtype)
        inside = jnp.where(here < blocks_dev - s, value, other)
        return jnp.where(here >= -s, inside, other)

    def block_of(ref, s, cols):
        value = ref[:blk, cols]
        for b in range(1, blocks_dev):
            value = jnp.where(at(value.shape[1]) == b - s, ref[b * blk : (b + 1) * blk, cols], value)
        return value

    def z_copy(s, j, half):
        part = pl.ds(half * z_rows, z_rows)
        return pltpu.make_async_remote_copy(
            src_ref=solved.at[s, j, part],
            dst_ref=arrived.at[s, j, part],
            send_sem=z_send.at[s, j, half],
            recv_sem=z_recv.at[s, j, half],
            device_id=(me, lax.rem(row + 1, n_row)),
            device_id_type=MESH,
        )

    def z_send_on(s, j, half):
        @pl.when(row < n_row - 1)
        def _():
            z_copy(s, j, half).start()

    def z_take(s, j, half):
        part = pl.ds(half * z_rows, z_rows)

        @pl.when(row > 0)
        def _():
            z_copy(s, j, half).wait_recv()
            solved[s, j, part, :] = own(s, solved[s, j, part, :], arrived[s, j, part, :])

    def dot(a, b):
        return jnp.dot(a, b, preferred_element_type=jnp.float32)

    def add_squares(s, j, value):
        sums = jnp.sum((value * value).reshape(blk // 8, 8, chunk), axis=0)
        square[j] = square[j] + own(s, sums, jnp.zeros_like(sums))

    def split_diag(s):
        full = diag_f32[s]
        high = full.astype(jnp.bfloat16)
        diag_hi[s] = high
        diag_lo[s] = (full - high.astype(jnp.float32)).astype(jnp.bfloat16)

    load_diag.wait()
    split_diag(0)
    square[...] = jnp.zeros_like(square)
    load_rows.wait()

    def columns(j):
        return slice(j * chunk, (j + 1) * chunk)

    for j in range(n_chunk):
        pending = block_of(rows_buf, 0, columns(j))
        value = dot(diag_hi[0], pending) + dot(diag_lo[0], pending)
        solved[0, j] = value.astype(jnp.bfloat16)
        add_squares(0, j, value)

        @pl.when(row == 0)
        def _():
            for half in range(HALVES):
                z_copy(0, j, half).start()

    split_diag(1)
    for cp in own_copies:
        cp.wait()

    def z_later(s, j, half):
        @pl.when(jnp.logical_and(row > 0, row < n_row - 1))
        def _():
            z_copy(s, j, half).start()

    z_units = n_chunk * HALVES

    for k in range(z_units):
        j, half = k // HALVES, k % HALVES
        z_take(0, j, half)
        z_later(0, j, half)
        if k == 0:
            f_action(0, 0)
        if k == z_units // 4:
            f_action(0, 1)
            f_start_own(1)
        if k == z_units // 2:
            f_action(0, 2)
    f_action(0, 3)
    cross[...] = block_of(fac[0], 1, slice(0, blk))

    def candidate(s, j):
        update = dot(cross[...], solved[0, j])
        pending = block_of(rows_buf, s, columns(j)).astype(jnp.float32) - update
        high = pending.astype(jnp.bfloat16)
        low = (pending - high.astype(jnp.float32)).astype(jnp.bfloat16)
        value = dot(diag_hi[s], high) + (dot(diag_lo[s], high) + dot(diag_hi[s], low))
        solved[s, j] = value.astype(jnp.bfloat16)
        add_squares(s, j, value)

    def finish(j):
        def body(b, _):
            rows = pl.ds(pl.multiple_of(b * blk, blk), blk)
            below = jnp.full((blk, chunk), b.astype(jnp.float32)).astype(jnp.bfloat16) - at(chunk)
            base = rows_buf[rows, columns(j)]
            update = dot(fac[0][rows, :], solved[0, j]) + dot(fac[1][rows, :], solved[1, j])
            moved = (base.astype(jnp.float32) - update).astype(jnp.bfloat16)
            value = jnp.where(below > 1, moved, base)
            value = jnp.where(below == 0, solved[0, j], value)
            value = jnp.where(below == 1, solved[1, j], value)
            out_ref[rows, columns(j)] = value
            return 0

        for part in range(2):
            lax.fori_loop(part * blocks_dev // 2, (part + 1) * blocks_dev // 2, body, 0)

    def v_copy(k):
        return pltpu.make_async_remote_copy(
            src_ref=square,
            dst_ref=square_in.at[k - 1],
            send_sem=v_send.at[k - 1],
            recv_sem=v_recv.at[k - 1],
            device_id=(me, lax.rem(row + k, n_row)),
            device_id_type=MESH,
        )

    done = 0
    for k in range(z_units):
        j, half = k // HALVES, k % HALVES
        if half == 0:
            candidate(1, j)
        z_take(1, j, half)
        z_send_on(1, j, half)
        if k == 0:
            f_action(1, 0)
        if k == z_units // 8:
            f_action(1, 1)
        if k == 3 * z_units // 8:
            f_action(1, 2)
        if k == z_units // 2:
            f_action(1, 3)
        if k == z_units - HALVES:
            for other in range(1, n_row):
                v_copy(other).start()
        if k >= z_units // 2:
            while done < j and done <= k - z_units // 2:
                finish(done)
                done += 1
    while done < n_chunk:
        finish(done)
        done += 1

    total = square[...]
    for other in range(1, n_row):
        v_copy(other).wait_recv()
        total = total + square_in[other - 1]
    for j in range(n_chunk):
        var_ref[:, columns(j)] = prior_ref[:, columns(j)] - jnp.sum(total[j], axis=0, keepdims=True)

    for s in range(steps):
        for rel in range(1, n_cand):
            for half in range(2):
                f_copy(s, rel, half).wait_send()

    @pl.when(row < n_row - 1)
    def _():
        for s in range(steps):
            for k in range(z_units):
                z_copy(s, k // HALVES, k % HALVES).wait_send()

    for other in range(1, n_row):
        v_copy(other).wait_send()


def write_kernel(src_ref, dst_ref, sems):
    parts = sems.shape[0]
    rows = src_ref.shape[0] // parts
    copies = [
        pltpu.make_async_copy(
            src_ref.at[pl.ds(p * rows, rows)], dst_ref.at[pl.ds(p * rows, rows)], sems.at[p]
        )
        for p in range(parts)
    ]
    for cp in copies:
        cp.start()
    for cp in copies:
        cp.wait()


def shards(n_cand, n_row, right_side, factor_panel, diag_inverse, prior_variance, block_index):
    rows_dev, cands = right_side.shape
    steps, blk = diag_inverse.shape[:2]
    chunk = 256
    n_chunk = cands // chunk
    bf16, f32 = jnp.bfloat16, jnp.float32
    any_space = pl.BlockSpec(memory_space=pl.ANY)
    vmem = pl.BlockSpec(memory_space=pltpu.VMEM)
    dma = pltpu.SemaphoreType.DMA
    out, variance = pl.pallas_call(
        functools.partial(kernel, n_cand, n_row, chunk),
        out_shape=(
            jax.ShapeDtypeStruct((rows_dev, cands), bf16),
            jax.ShapeDtypeStruct((1, cands), f32),
        ),
        in_specs=[any_space, any_space, any_space, vmem, pl.BlockSpec(memory_space=pltpu.SMEM)],
        out_specs=(vmem, vmem),
        scratch_shapes=[
            pltpu.VMEM((rows_dev, cands), bf16),
            pltpu.VMEM((rows_dev, blk), bf16),
            pltpu.VMEM((rows_dev, blk), bf16),
            pltpu.VMEM((steps, n_chunk, blk, chunk), bf16),
            pltpu.VMEM((steps, n_chunk, blk, chunk), bf16),
            pltpu.VMEM((steps, blk, blk), f32),
            pltpu.VMEM((steps, blk, blk), bf16),
            pltpu.VMEM((steps, blk, blk), bf16),
            pltpu.VMEM((blk, blk), bf16),
            pltpu.VMEM((blk, blk), bf16),
            pltpu.VMEM((n_chunk, 8, chunk), f32),
            pltpu.VMEM((n_row - 1, n_chunk, 8, chunk), f32),
            dma((2 + steps,)),
            dma((steps, n_cand, 2)),
            dma((steps, n_cand, 2)),
            dma((steps, n_chunk, HALVES)),
            dma((steps, n_chunk, HALVES)),
            dma((n_row - 1,)),
            dma((n_row - 1,)),
        ],
        compiler_params=pltpu.CompilerParams(
            collective_id=0, has_side_effects=True, vmem_limit_bytes=42 << 20
        ),
        cost_estimate=pl.CostEstimate(
            flops=2 * rows_dev * cands * steps * blk, bytes_accessed=32 << 20, transcendentals=0
        ),
        name="block_steps",
    )(right_side, factor_panel, diag_inverse, prior_variance.reshape(1, cands), block_index)
    written = pl.pallas_call(
        write_kernel,
        out_shape=jax.ShapeDtypeStruct(out.shape, out.dtype),
        in_specs=[any_space],
        out_specs=any_space,
        scratch_shapes=[dma((4,))],
        compiler_params=pltpu.CompilerParams(vmem_limit_bytes=4 << 20),
        name="write_rows",
    )(out)
    return written, variance.reshape(cands)


def solution(mesh):
    return jax.shard_map(
        functools.partial(shards, mesh.shape["cand"], mesh.shape["row"]),
        mesh=mesh,
        in_specs=(P("row", "cand"), P("row", "cand", None), P(), P("cand"), P()),
        out_specs=(P("row", "cand"), P("cand")),
        check_vma=False,
    )
```
